32 devices in a mesh: panel: 8 (over y, x, core), rep: 4 (over z).
Axes of the slice: x: 2, y: 2, z: 4, core: 2. Of those that a mesh axis runs over, the one named last changes fastest.
Arguments:
- user_cot: float32 [4096, 256], P('rep'), may hold values from -6 to 6
- item_cot: float32 [8192, 256], P('panel'), may hold values from -6 to 6
- tile_vals: float32 [8, 4, 40, 128, 128], P('panel', 'rep'), may hold values from 0 to 0.0191815, as said below
- tile_rows: int32 [8, 4, 40], P('panel', 'rep'), may hold values from 0 to 7
- tile_cols: int32 [8, 4, 40], P('panel', 'rep'), may hold values from 0 to 7
- tile_count: int32 [8, 4], P('panel', 'rep'), may hold values from 1 to 40, as said below
Outputs:
- grad_user: float32 [4096, 256], P(('rep', 'panel'))
- grad_item: float32 [8192, 256], P(('panel', 'rep'))
The draws below stay inside these ranges and needn't reach their ends.
Inputs may be any that keep to these rules, and one draw needn't show every extreme that they name: `tile_count`: at least one block has all 40 slots live. `tile_vals`: each tile has 2 to 10 percent nonzero entries; entries are nonnegative, near the inverse square root of a typical user degree times a typical item degree.
All inputs are finite; a program needn't handle non-finite values.
Results may differ from the reference program's by a relative error of at most 0.0001.
Values sent between devices are 32-bit elements; how exact they have to be, the bound alone decides.
No kernel may reach another device: no remote copies, remote signals or barrier semaphores. Data moves between devices by JAX's collectives and lax.ppermute only.
A program may use at most 64 MiB of HBM per device.

```python
import jax
import jax.numpy as jnp
from jax import lax

F = 256
TILE = 128
NT = 40
UB = 8
IB = 8
USERS = 4096
ITEMS = 8192
N_PANEL = 8
N_REP = 4


def draw_tile_count(key, part):
    heavy = jax.random.randint(jax.random.fold_in(key, 11), (N_PANEL, N_REP), 0, 8) == 0
    light = jax.random.randint(jax.random.fold_in(key, 12), (N_PANEL, N_REP), max(NT // 6, 1), NT // 2 + 1)
    counts = jnp.where(heavy, NT, light).reshape(-1)
    chosen = jax.random.randint(jax.random.fold_in(key, 13), (), 0, N_PANEL * N_REP)
    counts = counts.at[chosen].set(NT)
    return counts.reshape(N_PANEL, N_REP).astype(jnp.int32)


def draw_tile_vals(key, part):
    user_degree = 0.42 * NT * N_PANEL * TILE * 0.06 / UB
    item_degree = 0.42 * NT * N_REP * TILE * 0.06 / IB
    base_value = 1.0 / (user_degree * item_degree) ** 0.5
    density = jax.random.randint(jax.random.fold_in(key, 21), (N_PANEL, N_REP, NT, 1, 1), 20, 101)
    coins = jax.random.randint(jax.random.fold_in(key, 22), (N_PANEL, N_REP, NT, TILE, TILE), 0, 1000)
    present = (coins < density).astype(jnp.float32)
    factor = jax.random.uniform(jax.random.fold_in(key, 23), (N_PANEL, N_REP, NT, TILE, TILE), jnp.float32, 0.5, 1.5)
    return (present * factor * base_value).astype(jnp.float32)


def touch_ends(drawn, own_key, least, top_value):
    shape = drawn.shape
    index_at = [jax.random.randint(jax.random.fold_in(own_key, axis), (), 0, shape[axis]) for axis in range(len(shape))]
    drawn = drawn.at[tuple(index_at)].set(least)
    longest = shape.index(max(shape))
    index_at[longest] = (index_at[longest] + 1) % shape[longest]
    return drawn.at[tuple(index_at)].set(top_value)


def steps_of(rng, dims, cuts, smallest, top_value):
    level, own = 1.0, jax.random.fold_in(rng, 6)
    for position, shards_of in cuts:
        steps = jnp.exp(jax.random.uniform(jax.random.fold_in(own, position), (shards_of,), jnp.float32, smallest / len(cuts), top_value / len(cuts)))
        level = level * jnp.repeat(steps, dims[position] // shards_of).reshape([-1 if axis == position else 1 for axis in range(len(dims))])
    return level


def bell_draw(stream_key, shape, spread, most, shards=(), kind=jnp.bfloat16):
    values = spread * jax.random.normal(stream_key, shape, jnp.float32)
    if shards:
        values = values * steps_of(stream_key, shape, shards, -0.22, 0.18)
    return jnp.clip(values, -most, most).astype(kind)


def setup_inputs(seed: int = 0) -> dict:
    seeds = jax.random.split(jax.random.key(seed), 7)
    return {
        "user_cot": bell_draw(seeds[0], (USERS, F), 1.0, 6.0, ((0, 4),), jnp.float32),
        "item_cot": bell_draw(seeds[1], (ITEMS, F), 1.0, 6.0, ((0, 8),), jnp.float32),
        "tile_vals": draw_tile_vals(jax.random.fold_in(seeds[6], 71), 0),
        "tile_rows": touch_ends(jax.random.randint(seeds[3], (N_PANEL, N_REP, NT), 0, UB), jax.random.fold_in(seeds[3], 1), 0, UB - 1).astype(jnp.int32),
        "tile_cols": touch_ends(jax.random.randint(seeds[4], (N_PANEL, N_REP, NT), 0, IB), jax.random.fold_in(seeds[4], 1), 0, IB - 1).astype(jnp.int32),
        "tile_count": draw_tile_count(jax.random.fold_in(seeds[6], 71), 0),
    }


exact_mode = lax.Precision.HIGHEST


def reference(user_cot, item_cot, tile_vals, tile_rows, tile_cols, tile_count):
    feature = user_cot.shape[1]
    alive_mask = (jnp.arange(NT, dtype=jnp.int32)[None, None, :] < tile_count[:, :, None]).astype(tile_vals.dtype)
    row_hits = (tile_rows[..., None] == jnp.arange(UB, dtype=jnp.int32)[None, None, None, :]).astype(tile_vals.dtype) * alive_mask[..., None]
    col_hits = (tile_cols[..., None] == jnp.arange(IB, dtype=jnp.int32)[None, None, None, :]).astype(tile_vals.dtype) * alive_mask[..., None]

    def to_users(items):
        panels = items.reshape(N_PANEL, IB, TILE, feature)

        def one_panel(total, pieces):
            blocks, col_ids, hits, panel_items = pieces
            picked = jnp.take(panel_items, col_ids, axis=0)
            product = jnp.einsum("rtjk,rtkw->rtjw", blocks, picked, precision=exact_mode)
            return total + jnp.einsum("rtu,rtjw->rujw", hits, product, precision=exact_mode), None

        start = jnp.zeros((N_REP, UB, TILE, feature), items.dtype)
        total, ignored = lax.scan(one_panel, start, (tile_vals, tile_cols, row_hits, panels))
        return total.reshape(N_REP * UB * TILE, feature)

    def to_items(users):
        grouped = users.reshape(N_REP, UB, TILE, feature)

        def one_panel(pieces):
            blocks, row_ids, hits = pieces
            picked = jax.vmap(lambda group, index: jnp.take(group, index, axis=0))(grouped, row_ids)
            product = jnp.einsum("rtkj,rtkw->rtjw", blocks, picked, precision=exact_mode)
            return jnp.einsum("rti,rtjw->ijw", hits, product, precision=exact_mode)

        return lax.map(one_panel, (tile_vals, tile_rows, col_hits)).reshape(N_PANEL * IB * TILE, feature)

    user_third = user_cot / 3.0
    item_third = item_cot / 3.0
    item_mid = item_third + to_items(user_third)
    user_mid = user_third + to_users(item_third)
    grad_user = user_third + to_users(item_mid)
    grad_item = item_third + to_items(user_mid)
    return grad_user, grad_item
```

```python
import jax
import jax.numpy as jnp
from jax import lax
from jax.experimental import pallas as pl
from jax.experimental.pallas import tpu as pltpu
from jax.sharding import PartitionSpec as P

TILE = 128
BLOCK = 256
CHUNKS = 2
VMEM_BYTES = 48 * 1024 * 1024
THIRD = 1.0 / 3.0
NEAR = (((1,), (0,)), ((), ()))


def halves(values):
    high = values.astype(jnp.bfloat16)
    low = (values - high.astype(jnp.float32)).astype(jnp.bfloat16)
    return high, low


def product(left, right):
    dot = lambda a, b: lax.dot_general(a, b, NEAR, preferred_element_type=jnp.float32)
    return dot(left[0], right[0]) + (dot(left[0], right[1]) + dot(left[1], right[0]))


def add_to_items(high_ref, low_ref, users, items_ref):
    users_t = halves(users.T)
    step = min(BLOCK, high_ref.shape[1])
    for start in range(0, high_ref.shape[1], step):
        here = pl.ds(start, step)
        items_ref[here, :] = product(users_t, (high_ref[:, here], low_ref[:, here])).T


def build_kernel(count_ref, rows_ref, cols_ref, tiles_ref, users_ref, high_ref, low_ref, items_ref, whole_ref):
    whole_ref[...] = jnp.zeros_like(whole_ref)

    @pl.loop(0, count_ref[0, 0])
    def _(t):
        row = pl.ds(pl.multiple_of(rows_ref[0, t] * TILE, TILE), TILE)
        col = pl.ds(pl.multiple_of(cols_ref[0, t] * TILE, TILE), TILE)
        whole_ref[row, col] += tiles_ref[t]

    step = min(BLOCK, whole_ref.shape[0])
    for start in range(0, whole_ref.shape[0], step):
        here = pl.ds(start, step)
        high_ref[here, :], low_ref[here, :] = halves(whole_ref[here, :])
    add_to_items(high_ref, low_ref, users_ref[...] * THIRD, items_ref)


def items_kernel(high_ref, low_ref, users_ref, items_ref):
    add_to_items(high_ref, low_ref, users_ref[...], items_ref)


def users_kernel(scale, high_ref, low_ref, items_ref, users_ref):
    items = halves(items_ref[...] * scale)
    step = min(BLOCK, high_ref.shape[0])
    for start in range(0, high_ref.shape[0], step):
        here = pl.ds(start, step)
        users_ref[here, :] = product((high_ref[here, :], low_ref[here, :]), items)


def call(kernel, out_shape, ins, scratch=(), smem=0, flops=0, moved=0):
    vmem = pl.BlockSpec(memory_space=pltpu.VMEM)
    return pl.pallas_call(
        kernel,
        out_shape=out_shape,
        in_specs=[pl.BlockSpec(memory_space=pltpu.SMEM)] * smem + [vmem] * (len(ins) - smem),
        out_specs=jax.tree.map(lambda _: vmem, out_shape),
        scratch_shapes=list(scratch),
        compiler_params=pltpu.CompilerParams(vmem_limit_bytes=VMEM_BYTES),
        cost_estimate=pl.CostEstimate(flops=flops, bytes_accessed=moved, transcendentals=0),
    )(*ins)


def swap(values, n_panel):
    return lax.ppermute(values, "panel", [(i, i ^ 1) for i in range(n_panel)])


def line_ring(values, n_panel, n_rep):
    at = lambda p, r: p * n_rep + r
    pairs = []
    for p in range(0, n_panel, 2):
        for r in range(n_rep):
            pairs.append((at(p, r), at(p, r + 1) if r < n_rep - 1 else at(p + 1, r)))
            pairs.append((at(p + 1, r), at(p + 1, r - 1) if r > 0 else at(p, r)))
    return lax.ppermute(values, ("panel", "rep"), pairs)


def bits_of(n_panel):
    count = (n_panel // 2).bit_length() - 1
    turned = [(k + count // 2) % count for k in range(count)]
    return [(k + 1, turned[k] + 1) for k in range(count)]


def across(values, n_panel, bits):
    return lax.ppermute(values, "panel", [(i, i ^ (1 << bits[i & 1])) for i in range(n_panel)])


def pick(values, index, axis=0):
    return lax.dynamic_index_in_dim(values, index, axis, keepdims=False)


def per_device(user_cot, item_cot, tile_vals, tile_rows, tile_cols, tile_count):
    n_panel, n_rep = lax.axis_size("panel"), lax.axis_size("rep")
    panel, rep = lax.axis_index("panel"), lax.axis_index("rep")
    core = panel & 1
    place = jnp.where(core == 0, rep, n_rep - 1 - rep)
    real = lambda q: jnp.where(core == 0, q, n_rep - 1 - q)
    n_user, feature = user_cot.shape
    n_item = item_cot.shape[0]
    tiles = tile_vals[0, 0]
    f32 = lambda *shape: jax.ShapeDtypeStruct(shape, jnp.float32)
    b16 = lambda *shape: jax.ShapeDtypeStruct(shape, jnp.bfloat16)
    flops = 6 * n_user * n_item * feature
    moved = 4 * (n_user * n_item + 2 * n_user * feature)

    high, low, item_part = call(
        build_kernel,
        (b16(n_user, n_item), b16(n_user, n_item), f32(n_item, feature)),
        (tile_count, tile_rows[0], tile_cols[0], tiles, user_cot),
        [pltpu.VMEM((n_user, n_item), jnp.float32)],
        smem=3,
        flops=flops,
        moved=moved,
    )

    def to_items(users):
        return call(items_kernel, f32(n_item, feature), (high, low, users), flops=flops, moved=moved)

    def to_users(items, scale):
        kernel = lambda *refs: users_kernel(scale, *refs)
        return call(kernel, f32(n_user, feature), (high, low, items), flops=flops, moved=moved)

    chunk = n_item // n_rep // CHUNKS

    def slices(values):
        return values.reshape(n_rep, CHUNKS, chunk, feature)

    def both(mine, theirs, q, c):
        at = real(jnp.clip(q, 0, n_rep - 1))
        return jnp.stack([pick(mine, at)[c], pick(theirs, at)[c]])

    mine = slices(item_part)
    theirs = slices(swap(item_part, n_panel))
    held = [None] * CHUNKS
    for t in range(1, n_rep):
        for c in range(CHUNKS):
            sent = both(mine, theirs, place + n_rep - t, c)
            if t > 1:
                sent += jnp.where(place > 0, held[c], 0.0)
            held[c] = line_ring(sent, n_panel, n_rep)
    total = []
    for c in range(CHUNKS):
        part = jnp.where(place > 0, held[c], 0.0)
        total.append(part + swap(part, n_panel)[::-1] + both(mine, theirs, place, c))

    user_part = to_users(item_cot, THIRD).reshape(2, n_user // 2, feature)
    user_half = pick(user_part, core) + swap(pick(user_part, 1 - core), n_panel)
    for bits in bits_of(n_panel):
        user_half += across(user_half, n_panel, bits)
    other_half = swap(user_half, n_panel)
    user_sum = jnp.where(
        core == 0, jnp.concatenate([user_half, other_half]), jnp.concatenate([other_half, user_half])
    )

    again = to_items(user_sum)
    mine2 = slices(again)
    theirs2 = slices(swap(again, n_panel))
    came = [[] for _ in range(CHUNKS)]
    for t in range(1, n_rep + 1):
        for c in range(CHUNKS):
            if t == 1:
                sent = total[c]
            else:
                sent = jnp.where(place > 0, came[c][-1], 0.0) + jnp.where(
                    place >= t - 1, 0.0, both(mine2, theirs2, place + n_rep - (t - 1), c)
                )
            came[c].append(line_ring(sent, n_panel, n_rep))

    gathered = []
    for c in range(CHUNKS):
        near = jnp.stack([came[c][t][0] for t in range(n_rep - 1)])
        far = swap(jnp.stack([came[c][t][1] for t in range(n_rep - 1)]), n_panel)
        below, above = jnp.where(core == 0, near, far), jnp.where(core == 0, far, near)
        line = jnp.concatenate([below[::-1], total[c][:1], above])
        gathered.append(lax.dynamic_slice_in_dim(line, n_rep - 1 - rep, n_rep, 0))
    item_sum = jnp.stack(gathered, 1).reshape(n_item, feature)

    parts = to_users(item_sum, 1.0)
    bits = bits_of(n_panel)
    width = n_user // n_panel
    count = len(bits)
    parts = parts.reshape((n_panel // 2, 2, width, feature))
    scattered = pick(parts, core, 1) + swap(pick(parts, 1 - core, 1), n_panel)
    scattered = scattered.reshape((2,) * count + (width, feature))
    orders = [[count - b[k] for b in bits] for k in (0, 1)]
    scattered = jnp.where(
        core == 0,
        scattered.transpose(orders[0] + [count, count + 1]),
        scattered.transpose(orders[1] + [count, count + 1]),
    )
    for pair in bits:
        own = (panel >> jnp.where(core == 0, pair[0], pair[1])) & 1
        scattered = pick(scattered, own) + across(pick(scattered, 1 - own), n_panel, pair)

    own_users = lambda values: lax.dynamic_slice_in_dim(values, panel * width, width, 0)
    grad_user = own_users(user_cot) * THIRD + own_users(user_sum) + scattered

    pieces = []
    own_items = pick(slices(item_cot), rep)
    own_again = pick(mine2, rep)
    for c in range(CHUNKS):
        part = jnp.where(place > 0, came[c][-1], 0.0)
        pieces.append(
            own_items[c] * THIRD + total[c][0] + own_again[c] + part[0] + swap(part[1], n_panel)
        )
    grad_item = jnp.concatenate(pieces)
    return (grad_user, grad_item)


def solution(mesh):
    return jax.shard_map(
        per_device,
        mesh=mesh,
        in_specs=(
            P("rep", None),
            P("panel", None),
            P("panel", "rep", None, None, None),
            P("panel", "rep", None),
            P("panel", "rep", None),
            P("panel", "rep"),
        ),
        out_specs=(P(("rep", "panel"), None), P(("panel", "rep"), None)),
        check_vma=False,
    )
```

```python
import jax
import jax.numpy as jnp
from jax import lax
from jax.experimental import pallas as pl
from jax.experimental.pallas import tpu as pltpu
from jax.sharding import PartitionSpec as P

TILE = 128
BLOCK = 256
VMEM_BYTES = 20 * 1024 * 1024
THIRD = 1.0 / 3.0
NEAR = (((1,), (0,)), ((), ()))


def halves(values):
    high = values.astype(jnp.bfloat16)
    low = (values - high.astype(jnp.float32)).astype(jnp.bfloat16)
    return high, low


def product(left, right):
    dot = lambda a, b: lax.dot_general(a, b, NEAR, preferred_element_type=jnp.float32)
    return dot(left[0], right[0]) + (dot(left[0], right[1]) + dot(left[1], right[0]))


def blocks_of(size):
    step = min(BLOCK, size)
    return [pl.ds(start, step) for start in range(0, size, step)]


def build(count_ref, rows_ref, cols_ref, tiles_ref, whole_ref, high_ref, low_ref):
    whole_ref[...] = jnp.zeros_like(whole_ref)

    @pl.loop(0, count_ref[0, 0])
    def _(t):
        row = pl.ds(pl.multiple_of(rows_ref[0, t] * TILE, TILE), TILE)
        col = pl.ds(pl.multiple_of(cols_ref[0, t] * TILE, TILE), TILE)
        whole_ref[row, col] += tiles_ref[t]

    for here in blocks_of(whole_ref.shape[0]):
        high_ref[here, :], low_ref[here, :] = halves(whole_ref[here, :])


def transposed_product(high_ref, low_ref, users, full_ref, slice_refs):
    users_t = halves(users.T)
    for here in blocks_of(high_ref.shape[1]):
        full_ref[here, :] = product(users_t, (high_ref[:, here], low_ref[:, here])).T
    rep = lax.axis_index("rep")
    size = slice_refs[0].shape[0]
    for m, slice_ref in enumerate(slice_refs):
        slice_ref[...] = full_ref[pl.ds(pl.multiple_of((rep ^ m) * size, size), size), :]


def first_items_kernel(count_ref, rows_ref, cols_ref, tiles_ref, users_ref, high_ref, low_ref, *rest):
    *slice_refs, whole_ref, full_ref = rest
    build(count_ref, rows_ref, cols_ref, tiles_ref, whole_ref, high_ref, low_ref)
    transposed_product(high_ref, low_ref, users_ref[...] * THIRD, full_ref, slice_refs)


def user_block(chip, core, width):
    return pl.ds(pl.multiple_of((2 * chip + core) * width, width), width)


def second_items_kernel(high_ref, low_ref, mine_ref, other_ref, *rest):
    *slice_refs, users_ref, full_ref = rest
    core = lax.axis_index("panel") & 1
    for chip in range(mine_ref.shape[0]):
        width = mine_ref.shape[1]
        users_ref[user_block(chip, core, width), :] = mine_ref[chip]
        users_ref[user_block(chip, 1 - core, width), :] = other_ref[chip]
    transposed_product(high_ref, low_ref, users_ref[...], full_ref, slice_refs)


def users_product(high_ref, low_ref, items, full_ref):
    for here in blocks_of(high_ref.shape[0]):
        full_ref[here, :] = product((high_ref[here, :], low_ref[here, :]), items)


def first_users_kernel(high_ref, low_ref, items_ref, mine_ref, other_ref, full_ref):
    users_product(high_ref, low_ref, halves(items_ref[...] * THIRD), full_ref)
    core = lax.axis_index("panel") & 1
    chips, width = mine_ref.shape[:2]
    for chip in range(chips):
        mine_ref[chip] = full_ref[user_block(chip, core, width), :]
        other_ref[chip] = full_ref[user_block(chip, 1 - core, width), :]


def second_users_kernel(high_ref, low_ref, *rest):
    *slice_refs, mine_ref, other_ref, items_ref, full_ref = rest
    rep, panel = lax.axis_index("rep"), lax.axis_index("panel")
    size = slice_refs[0].shape[0]
    for m, slice_ref in enumerate(slice_refs):
        items_ref[pl.ds(pl.multiple_of((rep ^ m) * size, size), size), :] = slice_ref[...]
    users_product(high_ref, low_ref, halves(items_ref[...]), full_ref)
    core, place = panel & 1, panel >> 1
    chips, width = mine_ref.shape[:2]
    for m in range(chips):
        mine_ref[m] = full_ref[user_block(place ^ m, core, width), :]
        other_ref[m] = full_ref[user_block(place ^ m, 1 - core, width), :]


def call(kernel, out_shape, ins, scratch=(), smem=0, flops=0, moved=0):
    vmem = pl.BlockSpec(memory_space=pltpu.VMEM)
    return pl.pallas_call(
        kernel,
        out_shape=out_shape,
        in_specs=[pl.BlockSpec(memory_space=pltpu.SMEM)] * smem + [vmem] * (len(ins) - smem),
        out_specs=[vmem] * len(out_shape),
        scratch_shapes=list(scratch),
        compiler_params=pltpu.CompilerParams(vmem_limit_bytes=VMEM_BYTES),
        cost_estimate=pl.CostEstimate(flops=flops, bytes_accessed=moved, transcendentals=0),
    )(*ins)


def across_rep(values, bit):
    count = lax.axis_size("rep")
    return lax.ppermute(values, "rep", [(i, i ^ bit) for i in range(count)])


def across_panel(values, bits):
    count = lax.axis_size("panel")
    return lax.ppermute(values, "panel", [(i, i ^ bits[i & 1]) for i in range(count)])


def swap(values):
    return across_panel(values, (1, 1))


def low_bit(m):
    return m & -m


def scatter_sum(slices):
    parts = list(slices)
    order = sorted(range(1, len(parts)), key=lambda m: (low_bit(m), low_bit(m ^ low_bit(m)) or len(parts)))
    for m in order:
        target = m ^ low_bit(m)
        parts[target] = parts[target] + across_rep(parts[m], low_bit(m))
    return parts[0]


def gather(own):
    count = lax.axis_size("rep")
    known = {0: own}
    order = sorted(range(1, count), key=lambda m: (bin(m).count("1"), -m))
    for m in order:
        known[m] = across_rep(known[m ^ low_bit(m)], low_bit(m))
    return [known[m] for m in range(count)]


def per_device(user_cot, item_cot, tile_vals, tile_rows, tile_cols, tile_count):
    n_panel, n_rep = lax.axis_size("panel"), lax.axis_size("rep")
    panel, rep = lax.axis_index("panel"), lax.axis_index("rep")
    chips = n_panel // 2
    n_user, feature = user_cot.shape
    n_item = item_cot.shape[0]
    width, size = n_user // n_panel, n_item // n_rep
    f32 = lambda *shape: jax.ShapeDtypeStruct(shape, jnp.float32)
    b16 = lambda *shape: jax.ShapeDtypeStruct(shape, jnp.bfloat16)
    space = lambda *shape: pltpu.VMEM(shape, jnp.float32)
    item_slices = [f32(size, feature)] * n_rep
    user_blocks = [f32(chips, width, feature)] * 2
    cost = dict(
        flops=6 * n_user * n_item * feature,
        moved=4 * (n_user * n_item + 2 * n_user * feature),
    )

    high, low, *item_parts = call(
        first_items_kernel,
        [b16(n_user, n_item), b16(n_user, n_item)] + item_slices,
        (tile_count, tile_rows[0], tile_cols[0], tile_vals[0, 0], user_cot),
        [space(n_user, n_item), space(n_item, feature)],
        smem=3,
        **cost,
    )
    mine, other = call(
        first_users_kernel, user_blocks, (high, low, item_cot), [space(n_user, feature)], **cost
    )

    item_sum = scatter_sum(item_parts)

    mine = mine + swap(other)
    steps = (chips - 1).bit_length()
    for k in range(steps):
        mine = mine + across_panel(mine, (2 << k, 2 << ((k + steps // 2) % steps)))

    again = call(
        second_items_kernel,
        item_slices,
        (high, low, mine, swap(mine)),
        [space(n_user, feature), space(n_item, feature)],
        **cost,
    )
    gathered = gather(item_sum)
    last_mine, last_other = call(
        second_users_kernel,
        user_blocks,
        (high, low, *gathered),
        [space(n_item, feature), space(n_user, feature)],
        **cost,
    )

    last = last_mine + swap(last_other)
    grad_user = lax.dynamic_slice_in_dim(user_cot, panel * width, width, 0) * THIRD + (
        lax.dynamic_index_in_dim(mine, panel >> 1, 0, keepdims=False) + last[0]
    )
    for m in sorted(range(1, chips), key=lambda m: -m):
        grad_user = grad_user + across_panel(last[m], (2 * m, 2 * m))

    grad_item = lax.dynamic_slice_in_dim(item_cot, rep * size, size, 0) * THIRD + (
        item_sum + scatter_sum(again)
    )
    return (grad_user, grad_item)


def solution(mesh):
    return jax.shard_map(
        per_device,
        mesh=mesh,
        in_specs=(
            P("rep", None),
            P("panel", None),
            P("panel", "rep", None, None, None),
            P("panel", "rep", None),
            P("panel", "rep", None),
            P("panel", "rep"),
        ),
        out_specs=(P(("rep", "panel"), None), P(("panel", "rep"), None)),
        check_vma=False,
    )
```

```python
import functools

import jax
import jax.numpy as jnp
from jax import lax
from jax.experimental import pallas as pl
from jax.experimental.pallas import tpu as pltpu
from jax.sharding import PartitionSpec as P

TILE = 128
BLOCK = 256
COPIES = 4
VMEM_BYTES = 24 * 1024 * 1024
OFFSET = 2
COLLECT = 2
THIRD = 1.0 / 3.0
NEAR = (((1,), (0,)), ((), ()))


def halves(values):
    high = values.astype(jnp.bfloat16)
    low = (values - high.astype(jnp.float32)).astype(jnp.bfloat16)
    return high, low


def product(left, right):
    dot = lambda a, b: lax.dot_general(a, b, NEAR, preferred_element_type=jnp.float32)
    return dot(left[0], right[0]) + (dot(left[0], right[1]) + dot(left[1], right[0]))


def blocks_of(size):
    step = min(BLOCK, size)
    return [pl.ds(start, step) for start in range(0, size, step)]


def rows_at(index, size):
    return pl.ds(pl.multiple_of(index * size, size), size)


def item_product(high_ref, low_ref, users, items_ref):
    users_t = halves(users.T)
    for here in blocks_of(high_ref.shape[1]):
        items_ref[here, :] = product(users_t, (high_ref[:, here], low_ref[:, here])).T


def user_product(high_ref, low_ref, items, full_ref):
    for here in blocks_of(high_ref.shape[0]):
        full_ref[here, :] = product((high_ref[here, :], low_ref[here, :]), items)


def user_blocks(full_ref, mine_ref, other_ref, place):
    core = lax.axis_index("panel") & 1
    chips, width = mine_ref.shape[:2]
    for m in range(chips):
        mine_ref[m] = full_ref[rows_at(2 * (place ^ m) + core, width), :]
        other_ref[m] = full_ref[rows_at(2 * (place ^ m) + 1 - core, width), :]


def first_kernel(count_ref, rows_hbm, cols_hbm, tiles_hbm, users_hbm, items_hbm, *rest):
    high_ref, low_ref, sums_ref, mine_ref, other_ref = rest[:5]
    whole_ref, full_ref, tiles_ref, users_ref, items_ref, rows_ref, cols_ref, sems = rest[5:]
    index_copies = [
        pltpu.make_async_copy(source, target, sems.at[COPIES + 2 + k])
        for k, (source, target) in enumerate(((rows_hbm, rows_ref), (cols_hbm, cols_ref)))
    ]
    slots = tiles_ref.shape[0]
    steps = slots // COPIES if slots % COPIES == 0 else slots
    tile_copies = []
    for k, start in enumerate(range(0, slots, steps)):
        part = pl.ds(start, steps)
        tile_copies.append(pltpu.make_async_copy(tiles_hbm.at[0, 0, part], tiles_ref.at[part], sems.at[k]))
    users_copy = pltpu.make_async_copy(users_hbm, users_ref, sems.at[COPIES])
    items_copy = pltpu.make_async_copy(items_hbm, items_ref, sems.at[COPIES + 1])
    for copy in (*index_copies, *tile_copies, users_copy, items_copy):
        copy.start()

    whole_ref[...] = jnp.zeros_like(whole_ref)
    for copy in index_copies:
        copy.wait()
    for k, copy in enumerate(tile_copies):
        copy.wait()

        @pl.loop(k * steps, jnp.minimum((k + 1) * steps, count_ref[0, 0]))
        def _(t):
            whole_ref[rows_at(rows_ref[0, 0, t], TILE), rows_at(cols_ref[0, 0, t], TILE)] += tiles_ref[t]

    for here in blocks_of(whole_ref.shape[0]):
        high_ref[here, :], low_ref[here, :] = halves(whole_ref[here, :])
    users_copy.wait()
    item_product(high_ref, low_ref, users_ref[...] * THIRD, sums_ref)
    items_copy.wait()
    user_product(high_ref, low_ref, halves(items_ref[...] * THIRD), full_ref)
    user_blocks(full_ref, mine_ref, other_ref, 0)


def items_kernel(high_ref, low_ref, mine_ref, other_ref, sums_ref, users_ref):
    core = lax.axis_index("panel") & 1
    chips, width = mine_ref.shape[:2]
    for chip in range(chips):
        users_ref[rows_at(2 * chip + core, width), :] = mine_ref[chip]
        users_ref[rows_at(2 * chip + 1 - core, width), :] = other_ref[chip]
    item_product(high_ref, low_ref, users_ref[...], sums_ref)


def after(value, *others):
    return lax.optimization_barrier((value, others))[0] if others else value


def line_place(count):
    rep = lax.axis_index("rep")
    return jnp.where(lax.axis_index("panel") & 1 == 0, rep, count - 1 - rep)


def step_kernel(step, count, has_arrival, *refs):
    arrival_ref = refs[0] if has_arrival else None
    *sources, out_ref = refs[has_arrival:]
    size = out_ref.shape[0]
    place = line_place(count)
    index = step - 2 * place

    def put(ref, block):
        out_ref[...] = ref[rows_at(block, size), :]

    pl.when(index < count)(lambda: put(sources[0], jnp.maximum(index, 0)))
    if step >= count:
        pl.when((index >= count) & (index < 2 * count))(lambda: put(sources[1], index - count))
    if step >= 2 * count + OFFSET:
        unit = index - 2 * count - OFFSET
        target = jnp.clip(count - 1 - unit // 2, 0, count - 1)
        rep = jnp.where(lax.axis_index("panel") & 1 == 0, target, count - 1 - target)
        pl.when((unit >= 0) & (unit % 2 == 0))(lambda: put(sources[2], rep))
        pl.when((unit >= 0) & (unit % 2 == 1))(lambda: put(sources[3], rep))
    if has_arrival:

        @pl.when(place > 0)
        def _():
            out_ref[...] += arrival_ref[...]


def collect_kernel(*refs):
    *arrival_refs, out_ref = refs
    size = arrival_refs[0].shape[0]
    count = out_ref.shape[0] // size
    place = line_place(count)

    @pl.when(place == 0)
    def _():
        out_ref[...] = jnp.zeros_like(out_ref)

    for step, ref in enumerate(arrival_refs):
        block = step - 2 * (place - 1)

        @pl.when((place > 0) & (block >= 0) & (block < count))
        def _():
            out_ref[rows_at(block, size), :] = ref[...]


def users_kernel(user_cot_hbm, item_cot_hbm, high_ref, low_ref, sums_ref, far_ref, again_ref, users_ref, *rest):
    *arrival_refs, mine_ref, other_ref, own_ref, items_ref, full_ref, user_cot_ref, item_cot_ref, sems = rest
    panel, rep = lax.axis_index("panel"), lax.axis_index("rep")
    size, width = item_cot_ref.shape[0], user_cot_ref.shape[0]
    copies = (
        pltpu.make_async_copy(user_cot_hbm.at[rows_at(panel, width)], user_cot_ref, sems.at[0]),
        pltpu.make_async_copy(item_cot_hbm.at[rows_at(rep, size)], item_cot_ref, sems.at[1]),
    )
    for copy in copies:
        copy.start()
    count = items_ref.shape[0] // size
    place = line_place(count)
    items_ref[...] = sums_ref[...] + far_ref[...]
    for step, ref in enumerate(arrival_refs):
        block = step - 2 * (place - 1)

        @pl.when((place > 0) & (block >= 0) & (block < count))
        def _():
            items_ref[rows_at(block, size), :] += ref[...]

    user_product(high_ref, low_ref, halves(items_ref[...]), full_ref)
    user_blocks(full_ref, mine_ref, other_ref, panel >> 1)
    for copy in copies:
        copy.wait()
    mine_ref[0] += user_cot_ref[...] * THIRD + users_ref[panel >> 1]
    own_rows = rows_at(rep, size)
    own_ref[...] = item_cot_ref[...] * THIRD + (items_ref[own_rows, :] + again_ref[own_rows, :])


def call(kernel, out_shape, ins, scratch=(), spaces=(), flops=0, moved=0):
    spaces = list(spaces) + [pltpu.VMEM] * (len(ins) - len(spaces))
    return pl.pallas_call(
        kernel,
        out_shape=out_shape,
        in_specs=[pl.BlockSpec(memory_space=space) for space in spaces],
        out_specs=[pl.BlockSpec(memory_space=pltpu.VMEM)] * len(out_shape),
        scratch_shapes=list(scratch),
        compiler_params=pltpu.CompilerParams(vmem_limit_bytes=VMEM_BYTES),
        cost_estimate=pl.CostEstimate(flops=flops, bytes_accessed=moved, transcendentals=0),
    )(*ins)


def along_line(values):
    count, panels = lax.axis_size("rep"), lax.axis_size("panel")
    at = lambda p, r: p * count + r
    pairs = []
    for p in range(0, panels, 2):
        for r in range(count):
            pairs.append((at(p, r), at(p, r + 1) if r < count - 1 else at(p + 1, r)))
            pairs.append((at(p + 1, r), at(p + 1, r - 1) if r > 0 else at(p, r)))
    return lax.ppermute(values, ("panel", "rep"), pairs)


def across_panel(values, bits):
    count = lax.axis_size("panel")
    return lax.ppermute(values, "panel", [(i, i ^ bits[i & 1]) for i in range(count)])


def swap(values):
    return across_panel(values, (1, 1))


def per_device(user_cot, item_cot, tile_vals, tile_rows, tile_cols, tile_count):
    n_panel, n_rep = lax.axis_size("panel"), lax.axis_size("rep")
    panel, rep = lax.axis_index("panel"), lax.axis_index("rep")
    chips = n_panel // 2
    n_user, feature = user_cot.shape
    n_item = item_cot.shape[0]
    width, size = n_user // n_panel, n_item // n_rep
    f32 = lambda *shape: jax.ShapeDtypeStruct(shape, jnp.float32)
    b16 = lambda *shape: jax.ShapeDtypeStruct(shape, jnp.bfloat16)
    space = lambda *shape: pltpu.VMEM(shape, jnp.float32)
    cost = dict(
        flops=6 * n_user * n_item * feature,
        moved=4 * (n_user * n_item + 2 * n_user * feature),
    )
    items = f32(n_item, feature)
    blocks = [f32(chips, width, feature)] * 2
    piece = f32(size, feature)

    arguments = (tile_rows, tile_cols, tile_vals, user_cot, item_cot)
    pinned = [pltpu.with_memory_space_constraint(array, pltpu.HBM) for array in arguments]
    high, low, sums, mine, other = call(
        first_kernel,
        [b16(n_user, n_item), b16(n_user, n_item), items] + blocks,
        (tile_count, *pinned),
        [space(n_user, n_item), space(n_user, feature), space(*tile_vals.shape[2:])]
        + [space(n_user, feature), space(n_item, feature)]
        + [pltpu.SMEM(array.shape, jnp.int32) for array in arguments[:2]]
        + [pltpu.SemaphoreType.DMA((COPIES + 4,))],
        [pltpu.SMEM] + [pltpu.HBM] * 5,
        **cost,
    )

    sources = [swap(sums), sums]
    users = mine + swap(other)
    rounds = (chips - 1).bit_length()
    arrivals = []
    for step in range(4 * n_rep - 2 + OFFSET):
        if step == 2 * n_rep + OFFSET:
            for k in range(rounds):
                users = after(users, *arrivals[max(k - 1, 0) : k])
                with jax.named_scope(f"users_{k}"):
                    users = users + across_panel(users, (2 << k, 2 << ((k + rounds // 2) % rounds)))
            users = after(users, *arrivals[rounds - 1 : rounds])
            (again,) = call(items_kernel, [items], (high, low, users, swap(users)), [space(n_user, feature)], **cost)
            sources += [swap(again), again]
        before = arrivals[step - 2 : step - 1] if step >= 2 else []
        kernel = functools.partial(step_kernel, step, n_rep, len(before))
        used = sources[: 1 + (step >= n_rep)] if step < 2 * n_rep + OFFSET else sources
        (sent,) = call(kernel, [piece], (*before, *used))
        with jax.named_scope(f"line_{step}"):
            arrivals.append(along_line(sent))
        if step == 3 * n_rep - 5 + COLLECT:
            ready = after(arrivals[: 3 * n_rep - 4], *arrivals[3 * n_rep - 4 :])
            (passed,) = call(collect_kernel, [items], ready)
            far = swap(passed)

    last_mine, last_other, own_items = call(
        users_kernel,
        blocks + [piece],
        (*pinned[3:], high, low, sums, far, again, users, *arrivals[n_rep : 4 * n_rep - 4]),
        [space(n_item, feature), space(n_user, feature), space(width, feature), space(size, feature)]
        + [pltpu.SemaphoreType.DMA((2,))],
        [pltpu.HBM] * 2,
        **cost,
    )
    last = last_mine + swap(last_other)
    grad_user = last[0]
    for m in range(chips - 1, 0, -1):
        grad_user = grad_user + across_panel(last[m], (2 * m, 2 * m))

    place = line_place(n_rep)
    grad_item = own_items + jnp.where(place > 0, arrivals[-1], 0.0)
    grad_item = grad_item + jnp.where(place < n_rep - 1, swap(arrivals[-2]), 0.0)
    return (grad_user, grad_item)


def solution(mesh):
    return jax.shard_map(
        per_device,
        mesh=mesh,
        in_specs=(
            P("rep", None),
            P("panel", None),
            P("panel", "rep", None, None, None),
            P("panel", "rep", None),
            P("panel", "rep", None),
            P("panel", "rep"),
        ),
        out_specs=(P(("rep", "panel"), None), P(("panel", "rep"), None)),
        check_vma=False,
    )
```

```python
import functools

import jax
import jax.numpy as jnp
from jax import lax
from jax.experimental import pallas as pl
from jax.experimental.pallas import tpu as pltpu
from jax.sharding import PartitionSpec as P

TILE = 128
BLOCK = 256
COPIES = 4
VMEM_BYTES = 24 * 1024 * 1024
OFFSET = 2
COLLECT = 2
THIRD = 1.0 / 3.0
NEAR = (((1,), (0,)), ((), ()))


def halves(values):
    high = values.astype(jnp.bfloat16)
    low = (values - high.astype(jnp.float32)).astype(jnp.bfloat16)
    return high, low


def product(left, right):
    dot = lambda a, b: lax.dot_general(a, b, NEAR, preferred_element_type=jnp.float32)
    return dot(left[0], right[0]) + (dot(left[0], right[1]) + dot(left[1], right[0]))


def blocks_of(size):
    step = min(BLOCK, size)
    return [pl.ds(start, step) for start in range(0, size, step)]


def rows_at(index, size):
    return pl.ds(pl.multiple_of(index * size, size), size)


def item_product(high_ref, low_ref, users, items_ref):
    users_t = halves(users.T)
    for here in blocks_of(high_ref.shape[1]):
        items_ref[here, :] = product(users_t, (high_ref[:, here], low_ref[:, here])).T


def user_product(high_ref, low_ref, items, full_ref):
    for here in blocks_of(high_ref.shape[0]):
        full_ref[here, :] = product((high_ref[here, :], low_ref[here, :]), items)


def user_blocks(full_ref, mine_ref, other_ref, place):
    core = lax.axis_index("panel") & 1
    chips, width = mine_ref.shape[:2]
    for m in range(chips):
        mine_ref[m] = full_ref[rows_at(2 * (place ^ m) + core, width), :]
        other_ref[m] = full_ref[rows_at(2 * (place ^ m) + 1 - core, width), :]


def first_kernel(count_ref, rows_hbm, cols_hbm, tiles_hbm, users_hbm, items_hbm, *rest):
    high_ref, low_ref, sums_ref, mine_ref, other_ref = rest[:5]
    whole_ref, full_ref, tiles_ref, users_ref, items_ref, rows_ref, cols_ref, sems = rest[5:]
    index_copies = [
        pltpu.make_async_copy(source, target, sems.at[COPIES + 2 + k])
        for k, (source, target) in enumerate(((rows_hbm, rows_ref), (cols_hbm, cols_ref)))
    ]
    slots = tiles_ref.shape[0]
    steps = slots // COPIES if slots % COPIES == 0 else slots
    tile_copies = []
    for k, start in enumerate(range(0, slots, steps)):
        part = pl.ds(start, steps)
        tile_copies.append(pltpu.make_async_copy(tiles_hbm.at[0, 0, part], tiles_ref.at[part], sems.at[k]))
    users_copy = pltpu.make_async_copy(users_hbm, users_ref, sems.at[COPIES])
    items_copy = pltpu.make_async_copy(items_hbm, items_ref, sems.at[COPIES + 1])
    for copy in (*index_copies, *tile_copies, users_copy, items_copy):
        copy.start()

    whole_ref[...] = jnp.zeros_like(whole_ref)
    for copy in index_copies:
        copy.wait()
    for k, copy in enumerate(tile_copies):
        copy.wait()

        @pl.loop(k * steps, jnp.minimum((k + 1) * steps, count_ref[0, 0]))
        def _(t):
            whole_ref[rows_at(rows_ref[0, 0, t], TILE), rows_at(cols_ref[0, 0, t], TILE)] += tiles_ref[t]

    for here in blocks_of(whole_ref.shape[0]):
        high_ref[here, :], low_ref[here, :] = halves(whole_ref[here, :])
    users_copy.wait()
    item_product(high_ref, low_ref, users_ref[...] * THIRD, sums_ref)
    items_copy.wait()
    user_product(high_ref, low_ref, halves(items_ref[...] * THIRD), full_ref)
    user_blocks(full_ref, mine_ref, other_ref, 0)


def items_kernel(high_ref, low_ref, mine_ref, other_ref, sums_ref, users_ref):
    core = lax.axis_index("panel") & 1
    chips, width = mine_ref.shape[:2]
    for chip in range(chips):
        users_ref[rows_at(2 * chip + core, width), :] = mine_ref[chip]
        users_ref[rows_at(2 * chip + 1 - core, width), :] = other_ref[chip]
    item_product(high_ref, low_ref, users_ref[...], sums_ref)


def after(value, *others):
    return lax.optimization_barrier((value, others))[0] if others else value


def line_place(count):
    rep = lax.axis_index("rep")
    return jnp.where(lax.axis_index("panel") & 1 == 0, rep, count - 1 - rep)


def step_kernel(step, count, has_arrival, *refs):
    arrival_ref = refs[0] if has_arrival else None
    *sources, out_ref = refs[has_arrival:]
    size = out_ref.shape[0]
    place = line_place(count)
    index = step - 2 * place

    def put(ref, block):
        out_ref[...] = ref[rows_at(block, size), :]

    pl.when(index < count)(lambda: put(sources[0], jnp.maximum(index, 0)))
    if step >= count:
        pl.when((index >= count) & (index < 2 * count))(lambda: put(sources[1], index - count))
    if step >= 2 * count + OFFSET:
        unit = index - 2 * count - OFFSET
        target = jnp.clip(count - 1 - unit // 2, 0, count - 1)
        rep = jnp.where(lax.axis_index("panel") & 1 == 0, target, count - 1 - target)
        pl.when((unit >= 0) & (unit % 2 == 0))(lambda: put(sources[2], rep))
        pl.when((unit >= 0) & (unit % 2 == 1))(lambda: put(sources[3], rep))
    if has_arrival:

        @pl.when(place > 0)
        def _():
            out_ref[...] += arrival_ref[...]


def collect_kernel(*refs):
    *arrival_refs, out_ref = refs
    size = arrival_refs[0].shape[0]
    count = out_ref.shape[0] // size
    place = line_place(count)

    @pl.when(place == 0)
    def _():
        out_ref[...] = jnp.zeros_like(out_ref)

    for step, ref in enumerate(arrival_refs):
        block = step - 2 * (place - 1)

        @pl.when((place > 0) & (block >= 0) & (block < count))
        def _():
            out_ref[rows_at(block, size), :] = ref[...]


def users_kernel(user_cot_hbm, item_cot_hbm, high_ref, low_ref, sums_ref, far_ref, again_ref, users_ref, *rest):
    *arrival_refs, mine_ref, other_ref, own_ref, items_ref, full_ref, user_cot_ref, item_cot_ref, sems = rest
    panel, rep = lax.axis_index("panel"), lax.axis_index("rep")
    size, width = item_cot_ref.shape[0], user_cot_ref.shape[0]
    copies = (
        pltpu.make_async_copy(user_cot_hbm.at[rows_at(panel, width)], user_cot_ref, sems.at[0]),
        pltpu.make_async_copy(item_cot_hbm.at[rows_at(rep, size)], item_cot_ref, sems.at[1]),
    )
    for copy in copies:
        copy.start()
    count = items_ref.shape[0] // size
    place = line_place(count)
    items_ref[...] = sums_ref[...] + far_ref[...]
    for step, ref in enumerate(arrival_refs):
        block = step - 2 * (place - 1)

        @pl.when((place > 0) & (block >= 0) & (block < count))
        def _():
            items_ref[rows_at(block, size), :] += ref[...]

    user_product(high_ref, low_ref, halves(items_ref[...]), full_ref)
    user_blocks(full_ref, mine_ref, other_ref, panel >> 1)
    for copy in copies:
        copy.wait()
    mine_ref[0] += user_cot_ref[...] * THIRD + users_ref[panel >> 1]
    own_rows = rows_at(rep, size)
    own_ref[...] = item_cot_ref[...] * THIRD + (items_ref[own_rows, :] + again_ref[own_rows, :])


def call(kernel, out_shape, ins, scratch=(), spaces=(), flops=0, moved=0):
    spaces = list(spaces) + [pltpu.VMEM] * (len(ins) - len(spaces))
    return pl.pallas_call(
        kernel,
        out_shape=out_shape,
        in_specs=[pl.BlockSpec(memory_space=space) for space in spaces],
        out_specs=[pl.BlockSpec(memory_space=pltpu.VMEM)] * len(out_shape),
        scratch_shapes=list(scratch),
        compiler_params=pltpu.CompilerParams(vmem_limit_bytes=VMEM_BYTES),
        cost_estimate=pl.CostEstimate(flops=flops, bytes_accessed=moved, transcendentals=0),
    )(*ins)


def along_line(values):
    count, panels = lax.axis_size("rep"), lax.axis_size("panel")
    at = lambda p, r: p * count + r
    pairs = []
    for p in range(0, panels, 2):
        for r in range(count):
            pairs.append((at(p, r), at(p, r + 1) if r < count - 1 else at(p + 1, r)))
            pairs.append((at(p + 1, r), at(p + 1, r - 1) if r > 0 else at(p, r)))
    return lax.ppermute(values, ("panel", "rep"), pairs)


def across_panel(values, bits):
    count = lax.axis_size("panel")
    return lax.ppermute(values, "panel", [(i, i ^ bits[i & 1]) for i in range(count)])


def swap(values):
    return across_panel(values, (1, 1))


def per_device(user_cot, item_cot, tile_vals, tile_rows, tile_cols, tile_count):
    n_panel, n_rep = lax.axis_size("panel"), lax.axis_size("rep")
    panel, rep = lax.axis_index("panel"), lax.axis_index("rep")
    chips = n_panel // 2
    n_user, feature = user_cot.shape
    n_item = item_cot.shape[0]
    width, size = n_user // n_panel, n_item // n_rep
    f32 = lambda *shape: jax.ShapeDtypeStruct(shape, jnp.float32)
    b16 = lambda *shape: jax.ShapeDtypeStruct(shape, jnp.bfloat16)
    space = lambda *shape: pltpu.VMEM(shape, jnp.float32)
    cost = dict(
        flops=6 * n_user * n_item * feature,
        moved=4 * (n_user * n_item + 2 * n_user * feature),
    )
    items = f32(n_item, feature)
    blocks = [f32(chips, width, feature)] * 2
    piece = f32(size, feature)

    arguments = (tile_rows, tile_cols, tile_vals, user_cot, item_cot)
    pinned = [pltpu.with_memory_space_constraint(array, pltpu.HBM) for array in arguments]
    high, low, sums, mine, other = call(
        first_kernel,
        [b16(n_user, n_item), b16(n_user, n_item), items] + blocks,
        (tile_count, *pinned),
        [space(n_user, n_item), space(n_user, feature), space(*tile_vals.shape[2:])]
        + [space(n_user, feature), space(n_item, feature)]
        + [pltpu.SMEM(array.shape, jnp.int32) for array in arguments[:2]]
        + [pltpu.SemaphoreType.DMA((COPIES + 4,))],
        [pltpu.SMEM] + [pltpu.HBM] * 5,
        **cost,
    )

    users = mine + swap(other)
    sources = [swap(after(sums, users)), sums]
    rounds = (chips - 1).bit_length()
    arrivals = []
    for step in range(4 * n_rep - 2 + OFFSET):
        if step == 2 * n_rep + OFFSET:
            for k in range(rounds):
                users = after(users, *(arrivals[k : k + 1] if k else []))
                with jax.named_scope(f"users_{k}"):
                    users = users + across_panel(users, (2 << k, 2 << ((k + rounds // 2) % rounds)))
            users = after(users, *arrivals[rounds : rounds + 1])
            (again,) = call(items_kernel, [items], (high, low, users, swap(users)), [space(n_user, feature)], **cost)
            sources += [swap(again), again]
        before = arrivals[step - 2 : step - 1] if step >= 2 else []
        kernel = functools.partial(step_kernel, step, n_rep, len(before))
        used = sources[: 1 + (step >= n_rep)] if step < 2 * n_rep + OFFSET else sources
        (sent,) = call(kernel, [piece], (*before, *used))
        with jax.named_scope(f"line_{step}"):
            arrivals.append(along_line(sent))
        if step == 3 * n_rep - 5 + COLLECT:
            ready = after(arrivals[: 3 * n_rep - 4], *arrivals[3 * n_rep - 4 :])
            (passed,) = call(collect_kernel, [items], ready)
            far = swap(passed)

    last_mine, last_other, own_items = call(
        users_kernel,
        blocks + [piece],
        (*pinned[3:], high, low, sums, far, again, users, *arrivals[n_rep : 4 * n_rep - 4]),
        [space(n_item, feature), space(n_user, feature), space(width, feature), space(size, feature)]
        + [pltpu.SemaphoreType.DMA((2,))],
        [pltpu.HBM] * 2,
        **cost,
    )
    last = last_mine + swap(last_other)
    grad_user = last[0]
    for m in range(chips - 1, 0, -1):
        grad_user = grad_user + across_panel(last[m], (2 * m, 2 * m))

    place = line_place(n_rep)
    grad_item = own_items + jnp.where(place > 0, arrivals[-1], 0.0)
    grad_item = grad_item + jnp.where(place < n_rep - 1, swap(arrivals[-2]), 0.0)
    return (grad_user, grad_item)


def solution(mesh):
    return jax.shard_map(
        per_device,
        mesh=mesh,
        in_specs=(
            P("rep", None),
            P("panel", None),
            P("panel", "rep", None, None, None),
            P("panel", "rep", None),
            P("panel", "rep", None),
            P("panel", "rep"),
        ),
        out_specs=(P(("rep", "panel"), None), P(("panel", "rep"), None)),
        check_vma=False,
    )
```

```python
import functools

import jax
import jax.numpy as jnp
from jax import lax
from jax.experimental import pallas as pl
from jax.experimental.pallas import tpu as pltpu
from jax.sharding import PartitionSpec as P

TILE = 128
BLOCK = 256
COPIES = 4
VMEM_BYTES = 24 * 1024 * 1024
OFFSET = 2
COLLECT = 2
THIRD = 1.0 / 3.0
NEAR = (((1,), (0,)), ((), ()))


def halves(values):
    high = values.astype(jnp.bfloat16)
    low = (values - high.astype(jnp.float32)).astype(jnp.bfloat16)
    return high, low


def product(left, right):
    dot = lambda a, b: lax.dot_general(a, b, NEAR, preferred_element_type=jnp.float32)
    return dot(left[0], right[0]) + (dot(left[0], right[1]) + dot(left[1], right[0]))


def blocks_of(size):
    step = min(BLOCK, size)
    return [pl.ds(start, step) for start in range(0, size, step)]


def rows_at(index, size):
    return pl.ds(pl.multiple_of(index * size, size), size)


def item_product(high_ref, low_ref, users, items_ref):
    users_t = halves(users.T)
    for here in blocks_of(high_ref.shape[1]):
        items_ref[here, :] = product(users_t, (high_ref[:, here], low_ref[:, here])).T


def user_product(high_ref, low_ref, items, full_ref):
    for here in blocks_of(high_ref.shape[0]):
        full_ref[here, :] = product((high_ref[here, :], low_ref[here, :]), items)


def user_blocks(full_ref, mine_ref, other_ref, place):
    core = lax.axis_index("panel") & 1
    chips, width = mine_ref.shape[:2]
    for m in range(chips):
        mine_ref[m] = full_ref[rows_at(2 * (place ^ m) + core, width), :]
        other_ref[m] = full_ref[rows_at(2 * (place ^ m) + 1 - core, width), :]


def first_kernel(count_ref, rows_hbm, cols_hbm, tiles_hbm, users_hbm, items_hbm, *rest):
    high_ref, low_ref, users_ref, mine_ref, other_ref = rest[:5]
    whole_ref, full_ref, tiles_ref, items_ref, rows_ref, cols_ref, sems = rest[5:]
    index_copies = [
        pltpu.make_async_copy(source, target, sems.at[COPIES + 2 + k])
        for k, (source, target) in enumerate(((rows_hbm, rows_ref), (cols_hbm, cols_ref)))
    ]
    slots = tiles_ref.shape[0]
    steps = slots // COPIES if slots % COPIES == 0 else slots
    tile_copies = []
    for k, start in enumerate(range(0, slots, steps)):
        part = pl.ds(start, steps)
        tile_copies.append(pltpu.make_async_copy(tiles_hbm.at[0, 0, part], tiles_ref.at[part], sems.at[k]))
    users_copy = pltpu.make_async_copy(users_hbm, users_ref, sems.at[COPIES])
    items_copy = pltpu.make_async_copy(items_hbm, items_ref, sems.at[COPIES + 1])
    for copy in (*index_copies, *tile_copies, users_copy, items_copy):
        copy.start()

    whole_ref[...] = jnp.zeros_like(whole_ref)
    for copy in index_copies:
        copy.wait()
    for k, copy in enumerate(tile_copies):
        copy.wait()

        @pl.loop(k * steps, jnp.minimum((k + 1) * steps, count_ref[0, 0]))
        def _(t):
            whole_ref[rows_at(rows_ref[0, 0, t], TILE), rows_at(cols_ref[0, 0, t], TILE)] += tiles_ref[t]

    for here in blocks_of(whole_ref.shape[0]):
        high_ref[here, :], low_ref[here, :] = halves(whole_ref[here, :])
    items_copy.wait()
    user_product(high_ref, low_ref, halves(items_ref[...] * THIRD), full_ref)
    user_blocks(full_ref, mine_ref, other_ref, 0)
    users_copy.wait()


def sums_kernel(high_ref, low_ref, users_ref, sums_ref):
    item_product(high_ref, low_ref, users_ref[...] * THIRD, sums_ref)


def items_kernel(high_ref, low_ref, mine_ref, other_ref, sums_ref, users_ref):
    core = lax.axis_index("panel") & 1
    chips, width = mine_ref.shape[:2]
    for chip in range(chips):
        users_ref[rows_at(2 * chip + core, width), :] = mine_ref[chip]
        users_ref[rows_at(2 * chip + 1 - core, width), :] = other_ref[chip]
    item_product(high_ref, low_ref, users_ref[...], sums_ref)


def after(value, *others):
    return lax.optimization_barrier((value, others))[0] if others else value


def line_place(count):
    rep = lax.axis_index("rep")
    return jnp.where(lax.axis_index("panel") & 1 == 0, rep, count - 1 - rep)


def step_kernel(step, count, has_arrival, *refs):
    arrival_ref = refs[0] if has_arrival else None
    *sources, out_ref = refs[has_arrival:]
    size = out_ref.shape[0]
    place = line_place(count)
    index = step - 2 * place

    def put(ref, block):
        out_ref[...] = ref[rows_at(block, size), :]

    pl.when(index < count)(lambda: put(sources[0], jnp.maximum(index, 0)))
    if step >= count:
        pl.when((index >= count) & (index < 2 * count))(lambda: put(sources[1], index - count))
    if step >= 2 * count + OFFSET:
        unit = index - 2 * count - OFFSET
        target = jnp.clip(count - 1 - unit // 2, 0, count - 1)
        rep = jnp.where(lax.axis_index("panel") & 1 == 0, target, count - 1 - target)
        pl.when((unit >= 0) & (unit % 2 == 0))(lambda: put(sources[2], rep))
        pl.when((unit >= 0) & (unit % 2 == 1))(lambda: put(sources[3], rep))
    if has_arrival:

        @pl.when(place > 0)
        def _():
            out_ref[...] += arrival_ref[...]


def collect_kernel(*refs):
    *arrival_refs, out_ref = refs
    size = arrival_refs[0].shape[0]
    count = out_ref.shape[0] // size
    place = line_place(count)

    @pl.when(place == 0)
    def _():
        out_ref[...] = jnp.zeros_like(out_ref)

    for step, ref in enumerate(arrival_refs):
        block = step - 2 * (place - 1)

        @pl.when((place > 0) & (block >= 0) & (block < count))
        def _():
            out_ref[rows_at(block, size), :] = ref[...]


def users_kernel(user_cot_hbm, item_cot_hbm, high_ref, low_ref, sums_ref, far_ref, again_ref, users_ref, *rest):
    *arrival_refs, mine_ref, other_ref, own_ref, items_ref, full_ref, user_cot_ref, item_cot_ref, sems = rest
    panel, rep = lax.axis_index("panel"), lax.axis_index("rep")
    size, width = item_cot_ref.shape[0], user_cot_ref.shape[0]
    copies = (
        pltpu.make_async_copy(user_cot_hbm.at[rows_at(panel, width)], user_cot_ref, sems.at[0]),
        pltpu.make_async_copy(item_cot_hbm.at[rows_at(rep, size)], item_cot_ref, sems.at[1]),
    )
    for copy in copies:
        copy.start()
    count = items_ref.shape[0] // size
    place = line_place(count)
    items_ref[...] = sums_ref[...] + far_ref[...]
    for step, ref in enumerate(arrival_refs):
        block = step - 2 * (place - 1)

        @pl.when((place > 0) & (block >= 0) & (block < count))
        def _():
            items_ref[rows_at(block, size), :] += ref[...]

    user_product(high_ref, low_ref, halves(items_ref[...]), full_ref)
    user_blocks(full_ref, mine_ref, other_ref, panel >> 1)
    for copy in copies:
        copy.wait()
    mine_ref[0] += user_cot_ref[...] * THIRD + users_ref[panel >> 1]
    own_rows = rows_at(rep, size)
    own_ref[...] = item_cot_ref[...] * THIRD + (items_ref[own_rows, :] + again_ref[own_rows, :])


def call(kernel, out_shape, ins, scratch=(), spaces=(), flops=0, moved=0):
    spaces = list(spaces) + [pltpu.VMEM] * (len(ins) - len(spaces))
    return pl.pallas_call(
        kernel,
        out_shape=out_shape,
        in_specs=[pl.BlockSpec(memory_space=space) for space in spaces],
        out_specs=[pl.BlockSpec(memory_space=pltpu.VMEM)] * len(out_shape),
        scratch_shapes=list(scratch),
        compiler_params=pltpu.CompilerParams(vmem_limit_bytes=VMEM_BYTES),
        cost_estimate=pl.CostEstimate(flops=flops, bytes_accessed=moved, transcendentals=0),
    )(*ins)


def along_line(values):
    count, panels = lax.axis_size("rep"), lax.axis_size("panel")
    at = lambda p, r: p * count + r
    pairs = []
    for p in range(0, panels, 2):
        for r in range(count):
            pairs.append((at(p, r), at(p, r + 1) if r < count - 1 else at(p + 1, r)))
            pairs.append((at(p + 1, r), at(p + 1, r - 1) if r > 0 else at(p, r)))
    return lax.ppermute(values, ("panel", "rep"), pairs)


def across_panel(values, bits):
    count = lax.axis_size("panel")
    return lax.ppermute(values, "panel", [(i, i ^ bits[i & 1]) for i in range(count)])


def swap(values):
    return across_panel(values, (1, 1))


def per_device(user_cot, item_cot, tile_vals, tile_rows, tile_cols, tile_count):
    n_panel, n_rep = lax.axis_size("panel"), lax.axis_size("rep")
    panel, rep = lax.axis_index("panel"), lax.axis_index("rep")
    chips = n_panel // 2
    n_user, feature = user_cot.shape
    n_item = item_cot.shape[0]
    width, size = n_user // n_panel, n_item // n_rep
    f32 = lambda *shape: jax.ShapeDtypeStruct(shape, jnp.float32)
    b16 = lambda *shape: jax.ShapeDtypeStruct(shape, jnp.bfloat16)
    space = lambda *shape: pltpu.VMEM(shape, jnp.float32)
    cost = dict(
        flops=6 * n_user * n_item * feature,
        moved=4 * (n_user * n_item + 2 * n_user * feature),
    )
    items = f32(n_item, feature)
    blocks = [f32(chips, width, feature)] * 2
    piece = f32(size, feature)

    arguments = (tile_rows, tile_cols, tile_vals, user_cot, item_cot)
    pinned = [pltpu.with_memory_space_constraint(array, pltpu.HBM) for array in arguments]
    high, low, held, mine, other = call(
        first_kernel,
        [b16(n_user, n_item), b16(n_user, n_item), f32(n_user, feature)] + blocks,
        (tile_count, *pinned),
        [space(n_user, n_item), space(n_user, feature), space(*tile_vals.shape[2:])]
        + [space(n_item, feature)]
        + [pltpu.SMEM(array.shape, jnp.int32) for array in arguments[:2]]
        + [pltpu.SemaphoreType.DMA((COPIES + 4,))],
        [pltpu.SMEM] + [pltpu.HBM] * 5,
        **cost,
    )

    (sums,) = call(sums_kernel, [items], (high, low, held), **cost)
    users = mine + swap(other)
    sources = [swap(after(sums, users)), sums]
    rounds = (chips - 1).bit_length()
    arrivals = []
    for step in range(4 * n_rep - 2 + OFFSET):
        if step == 2 * n_rep + OFFSET:
            for k in range(rounds):
                users = after(users, *(arrivals[k : k + 1] if k else []))
                with jax.named_scope(f"users_{k}"):
                    users = users + across_panel(users, (2 << k, 2 << ((k + rounds // 2) % rounds)))
            users = after(users, *arrivals[rounds : rounds + 1])
            (again,) = call(items_kernel, [items], (high, low, users, swap(users)), [space(n_user, feature)], **cost)
            sources += [swap(again), again]
        before = arrivals[step - 2 : step - 1] if step >= 2 else []
        kernel = functools.partial(step_kernel, step, n_rep, len(before))
        used = sources[: 1 + (step >= n_rep)] if step < 2 * n_rep + OFFSET else sources
        (sent,) = call(kernel, [piece], (*before, *used))
        with jax.named_scope(f"line_{step}"):
            arrivals.append(along_line(sent))
        if step == 3 * n_rep - 5 + COLLECT:
            ready = after(arrivals[: 3 * n_rep - 4], *arrivals[3 * n_rep - 4 :])
            (passed,) = call(collect_kernel, [items], ready)
            far = swap(passed)

    last_mine, last_other, own_items = call(
        users_kernel,
        blocks + [piece],
        (*pinned[3:], high, low, sums, far, again, users, *arrivals[n_rep : 4 * n_rep - 4]),
        [space(n_item, feature), space(n_user, feature), space(width, feature), space(size, feature)]
        + [pltpu.SemaphoreType.DMA((2,))],
        [pltpu.HBM] * 2,
        **cost,
    )
    last = last_mine + swap(last_other)
    grad_user = last[0]
    for m in range(chips - 1, 0, -1):
        grad_user = grad_user + across_panel(last[m], (2 * m, 2 * m))

    place = line_place(n_rep)
    grad_item = own_items + jnp.where(place > 0, arrivals[-1], 0.0)
    grad_item = grad_item + jnp.where(place < n_rep - 1, swap(arrivals[-2]), 0.0)
    return (grad_user, grad_item)


def solution(mesh):
    return jax.shard_map(
        per_device,
        mesh=mesh,
        in_specs=(
            P("rep", None),
            P("panel", None),
            P("panel", "rep", None, None, None),
            P("panel", "rep", None),
            P("panel", "rep", None),
            P("panel", "rep"),
        ),
        out_specs=(P(("rep", "panel"), None), P(("panel", "rep"), None)),
        check_vma=False,
    )
```
